1024 devices in a mesh: fsdp: 128 (over z_lo, y, x), tensor: 8 (over z_hi, core).
Axes of the slice: x: 8, y: 8, z: 8 (z_hi: 4, z_lo: 2; z = z_hi * 2 + z_lo), core: 2. Of those that a mesh axis runs over, the one named last changes fastest.
Arguments:
- tokens: bfloat16 [16384, 16384], P('fsdp', 'tensor'), may hold values from -6 to 6
- seg_ids: int32 [128, 128], P('fsdp'), may hold values from 0 to 7, never falling along the last dimension, each value on 1 to 64 neighbouring positions
- key_weight: bfloat16 [512, 16384], P('fsdp', 'tensor'), may hold values from -0.046875 to 0.046875
- key_grad: bfloat16 [16384, 512], P('fsdp'), may hold values from -24 to 24
Outputs:
- keys: bfloat16 [16384, 512], P('fsdp')
- grad_tokens: bfloat16 [16384, 16384], P('fsdp', 'tensor')
- grad_key_weight: float32 [512, 16384], P('fsdp', 'tensor')
The draws below stay inside these ranges and needn't reach their ends.
Inputs may be any that keep to these rules, and one draw needn't show every extreme that they name: `seg_ids`: within each window the ids never fall; each document spans 1 to 64 tokens, one exactly 64.
All inputs are finite; a program needn't handle non-finite values.
Results may differ from the reference program's by a relative error of at most 0.0041.
Values may be sent and summed in bfloat16 or wider, within the bound.
No kernel may reach another device: no remote copies, remote signals or barrier semaphores. Data moves between devices by JAX's collectives and lax.ppermute only.
A program may use at most 32 MiB of HBM per device.

```python
import math
import jax
import jax.numpy as jnp
import numpy as np
from jax import lax

D = 16384
KV_HEADS = 4
HEAD = 128
TOK_DEV = 128
TOKENS = 16384
N_FSDP = 128


def strengthened(values, key, source, target, shards_of, factor):
    owner, partner = [(jnp.arange(values.shape[position]) // (values.shape[position] // shards_of)).reshape([-1 if axis == position else 1 for axis in range(values.ndim)]) for position in (source, target)]
    chosen = jax.random.permutation(key, shards_of)[partner]
    strong = (owner == chosen) | (owner == (partner + shards_of // 2) % shards_of)
    return jnp.where(strong, factor * values, values)


def level_of(stream_key, dims, pieces, least, high):
    loudness, own = 1.0, jax.random.fold_in(stream_key, 6)
    for axis_at, shards_of in pieces:
        draws = jnp.exp(jax.random.uniform(jax.random.fold_in(own, axis_at), (shards_of,), jnp.float32, least / len(pieces), high / len(pieces)))
        loudness = loudness * jnp.repeat(draws, dims[axis_at] // shards_of).reshape([-1 if axis == axis_at else 1 for axis in range(len(dims))])
    return loudness


def split_up(amount, total, limit, lean):
    loads = [(1 << 20) // math.isqrt(rank ** lean) + 1 for rank in range(2, amount + 1)]
    spare, counts = total - limit - (amount - 1), [1] * (amount - 1)
    while spare > 0:
        candidates = [i for i in range(amount - 1) if counts[i] < limit]
        pool, remaining = sum([loads[i] for i in candidates]), spare
        for i in candidates:
            extra = min(limit - counts[i], max(1, remaining * loads[i] // pool), spare)
            counts[i] = counts[i] + extra
            spare = spare - extra
    return np.array([limit] + counts)


def uneven(key, count, total, limit, skew):
    if count == 2:
        one = jax.random.randint(key, (), max(1, total - limit), min(limit, total - 1) + 1)
        return jnp.stack([one, total - one])
    sizes = jnp.asarray(split_up(count, total, limit, skew), jnp.int32)
    pairs = (count - 1) // 2
    donor, sink = sizes[1:1 + 2 * pairs:2], sizes[2:2 + 2 * pairs:2]
    margin = jnp.minimum(donor - 1, limit - sink)
    shifted = jax.random.randint(jax.random.fold_in(key, 1), (pairs,), 0, 1 << 20) % (margin + 1)
    sizes = sizes.at[1:1 + 2 * pairs:2].set(donor - shifted).at[2:2 + 2 * pairs:2].set(sink + shifted)
    return sizes[jax.random.permutation(jax.random.fold_in(key, 2), count)]


def centred(stream_key, dims, scale, reach, pieces=(), kind=jnp.bfloat16):
    result = jax.random.normal(stream_key, dims, jnp.float32) * scale
    if len(pieces) > 0:
        result = level_of(stream_key, dims, pieces, -0.22, 0.18) * result
    return jnp.clip(result, min=-reach, max=reach).astype(kind)


def bell_draw_with(stream_key, extent, spread, most, shards, heavy, kind=jnp.bfloat16):
    drawn = spread * jax.random.normal(stream_key, extent, jnp.float32)
    if shards:
        drawn = drawn * level_of(stream_key, extent, shards, -0.22, 0.18)
    return jnp.clip(strengthened(drawn, jax.random.fold_in(stream_key, 3), *heavy), -most, most).astype(kind)


def setup_inputs(seed: int = 0) -> dict:
    splits = jax.random.split(jax.random.key(seed), 5)
    tokens = centred(splits[0], (TOKENS, D), 1.0, 6.0, ((0, 128), (1, 8)))
    seg_ids = jax.vmap(lambda own: jnp.searchsorted(jnp.cumsum(uneven(own, 8, TOK_DEV, TOK_DEV // 2, 2)), jnp.arange(TOK_DEV), side="right"))(jax.random.split(splits[1], N_FSDP)).reshape((N_FSDP, TOK_DEV)).astype(jnp.int32)
    key_weight = centred(splits[2], (KV_HEADS * HEAD, D), D ** -0.5, 0.046875, ((0, 128), (1, 8)))
    key_grad = bell_draw_with(splits[3], (TOKENS, KV_HEADS * HEAD), 1.0, 24.0, ((0, 128),), (0, 1, 128, 5.5))
    return {"tokens": tokens, "seg_ids": seg_ids, "key_weight": key_weight, "key_grad": key_grad}


def doc_positions(seg_ids):
    width = seg_ids.shape[1]
    index = jnp.arange(width, dtype=jnp.int32)
    change = jnp.concatenate([jnp.ones((seg_ids.shape[0], 1), bool), seg_ids[:, 1:] != seg_ids[:, :-1]], axis=1)
    first = lax.cummax(jnp.where(change, index[None, :], 0).astype(jnp.int32), axis=1)
    return (index[None, :] - first).reshape(-1)


def angles(positions, half):
    freq = 500000.0 ** (-2.0 * jnp.arange(half, dtype=jnp.float32) / (2 * half))
    turn = positions.astype(jnp.float32)[:, None] * freq[None, :]
    return jnp.cos(turn)[:, None, :], jnp.sin(turn)[:, None, :]


def rotate(field, cosine, sine, sign):
    rows = field.shape[0]
    shaped = field.reshape(rows, -1, HEAD)
    first, second = shaped[..., :HEAD // 2], shaped[..., HEAD // 2:]
    out = jnp.concatenate([first * cosine - sign * second * sine, second * cosine + sign * first * sine], axis=-1)
    return out.reshape(rows, -1)


def reference(tokens, seg_ids, key_weight, key_grad):
    cosine, sine = angles(doc_positions(seg_ids), HEAD // 2)
    kraw = lax.dot_general(tokens, key_weight, (((1,), (1,)), ((), ())), preferred_element_type=jnp.float32)
    keys = rotate(kraw, cosine, sine, 1.0).astype(jnp.bfloat16)
    kback = rotate(key_grad.astype(jnp.float32), cosine, sine, -1.0).astype(jnp.bfloat16)
    grad_tokens = jnp.dot(kback, key_weight, preferred_element_type=jnp.float32).astype(jnp.bfloat16)
    grad_key_weight = lax.dot_general(kback, tokens, (((0,), (0,)), ((), ())), preferred_element_type=jnp.float32)
    return keys, grad_tokens, grad_key_weight
```

```python
import jax
import jax.numpy as jnp
from jax import lax
from jax.sharding import Mesh, PartitionSpec as P

HEAD = 128
SWAP = ((0, 1), (1, 0))


def doc_positions(segments):
    width = segments.shape[0]
    index = jnp.arange(width, dtype=jnp.int32)
    change = jnp.concatenate([jnp.ones((1,), bool), segments[1:] != segments[:-1]])
    first = lax.cummax(jnp.where(change, index, 0))
    return index - first


def angles(positions, half):
    freq = 500000.0 ** (-2.0 * jnp.arange(half, dtype=jnp.float32) / (2 * half))
    turn = positions.astype(jnp.float32)[:, None] * freq[None, :]
    return (jnp.cos(turn)[:, None, :], jnp.sin(turn)[:, None, :])


def rotate(field, cosine, sine, sign):
    rows = field.shape[0]
    shaped = field.reshape(rows, -1, HEAD)
    first, second = (shaped[..., : HEAD // 2], shaped[..., HEAD // 2 :])
    out = jnp.concatenate(
        [first * cosine - sign * second * sine, second * cosine + sign * first * sine], axis=-1
    )
    return out.reshape(rows, -1)


def dot(a, b, da, db):
    return lax.dot_general(a, b, (((da,), (db,)), ((), ())), preferred_element_type=jnp.float32)


def body(tokens, seg_ids, key_weight, key_grad):
    bf16 = jnp.bfloat16
    zl = lax.axis_index("zl")
    t = lax.axis_index("zh") * 2 + lax.axis_index("c")
    spread = jnp.broadcast_to(key_weight[None], (64, 4, 2048))
    gathered = lax.all_to_all(spread, ("y", "x"), 0, 0)
    tok_p = lax.ppermute(tokens, "zl", SWAP)

    cosine, sine = angles(doc_positions(seg_ids[0]), HEAD // 2)
    kback = rotate(key_grad.astype(jnp.float32), cosine, sine, -1.0).astype(bf16)
    left, right = kback[:, :256], kback[:, 256:]
    kb_p = lax.ppermute(jnp.where(zl == 0, right, left), "zl", SWAP)
    kb = jnp.where(zl == 0, left, right)

    partial = (dot(kb, tokens, 0, 0) + dot(kb_p, tok_p, 0, 0)).astype(bf16)
    gathered, partial = lax.optimization_barrier((gathered, partial))
    scattered = lax.all_to_all(partial.reshape(64, 4, 2048), ("y", "x"), 0, 0)

    weights = gathered.reshape(256, 2048)
    k_own = dot(tokens, weights, 1, 1).astype(bf16)
    k_par = dot(tok_p, weights, 1, 1).astype(bf16)
    ks = jnp.where(zl == 0, jnp.stack([k_own, k_par]), jnp.stack([k_par, k_own]))
    ks = lax.all_to_all(ks.reshape(16, 16, 256), ("zl", "zh", "c"), 0, 0)

    g_par = lax.ppermute(dot(kb_p, weights, 1, 0).astype(bf16), "zl", SWAP)
    grad_tokens = (dot(kb, weights, 1, 0) + g_par.astype(jnp.float32)).astype(bf16)

    kraw = jnp.sum(ks.reshape(2, 8, 16, 256).astype(jnp.float32), axis=1)
    kraw = kraw.transpose(1, 0, 2).reshape(16, 512)
    own_cos = lax.dynamic_slice_in_dim(cosine, t * 16, 16, 0)
    own_sin = lax.dynamic_slice_in_dim(sine, t * 16, 16, 0)
    keys = rotate(kraw, own_cos, own_sin, 1.0).astype(bf16)
    keys = lax.all_to_all(jnp.broadcast_to(keys[None], (8, 16, 512)), ("zh", "c"), 0, 0)
    keys = keys.reshape(128, 512)

    grad_key_weight = jnp.sum(scattered.astype(jnp.float32), axis=0)
    return keys, grad_tokens, grad_key_weight


def solution(mesh):
    fine = Mesh(mesh.devices.reshape(2, 8, 8, 4, 2), ("zl", "y", "x", "zh", "c"))
    fsdp, tensor = ("zl", "y", "x"), ("zh", "c")
    placed = (P(fsdp, tensor), P(fsdp, None), P(fsdp, tensor), P(fsdp, None))
    return jax.shard_map(
        body,
        mesh=fine,
        in_specs=placed,
        out_specs=(P(fsdp, None), P(fsdp, tensor), P(fsdp, tensor)),
        check_vma=False,
    )
```

```python
import jax
import jax.numpy as jnp
from jax import lax
from jax.sharding import Mesh, PartitionSpec as P

HEAD = 128
SWAP = ((0, 1), (1, 0))


def doc_positions(segments):
    index = jnp.arange(segments.shape[0], dtype=jnp.int32)
    return index - jnp.sum((segments[None, :] < segments[:, None]).astype(jnp.int32), axis=1)


def angles(positions, half):
    freq = 500000.0 ** (-2.0 * jnp.arange(half, dtype=jnp.float32) / (2 * half))
    turn = positions.astype(jnp.float32)[:, None] * freq[None, :]
    return (jnp.cos(turn)[:, None, :], jnp.sin(turn)[:, None, :])


def rotate(field, cosine, sine, sign):
    rows = field.shape[0]
    shaped = field.reshape(rows, -1, HEAD)
    first, second = (shaped[..., : HEAD // 2], shaped[..., HEAD // 2 :])
    out = jnp.concatenate(
        [first * cosine - sign * second * sine, second * cosine + sign * first * sine], axis=-1
    )
    return out.reshape(rows, -1)


def dot(a, b, da, db):
    return lax.dot_general(a, b, (((da,), (db,)), ((), ())), preferred_element_type=jnp.float32)


def body(tokens, seg_ids, key_weight, key_grad):
    bf16, f32 = jnp.bfloat16, jnp.float32
    zl, core = lax.axis_index("zl"), lax.axis_index("c")
    spread = jnp.broadcast_to(key_weight[None], (64, 4, 2048))
    gathered = lax.all_to_all(spread, ("y", "x"), 0, 0)
    tok_p = lax.ppermute(tokens, "zl", SWAP)

    cosine, sine = angles(doc_positions(seg_ids[0]), HEAD // 2)
    kback = rotate(key_grad.astype(f32), cosine, sine, -1.0).astype(bf16)
    left, right = kback[:, :256], kback[:, 256:]
    kb_p = lax.ppermute(jnp.where(zl == 0, right, left), "zl", SWAP)
    kb = jnp.where(zl == 0, left, right)

    partial = (dot(kb, tokens, 0, 0) + dot(kb_p, tok_p, 0, 0)).astype(bf16)

    weights = gathered.reshape(256, 2048)
    k_own, k_par = dot(tokens, weights, 1, 1), dot(tok_p, weights, 1, 1)
    mine = core * 64
    other = 64 - mine
    cut = lambda field, at: lax.dynamic_slice_in_dim(field, at, 64, 0)
    keep = cut(k_own, mine)
    to_c, to_z, to_d = cut(k_own, other), cut(k_par, mine), cut(k_par, other)
    to_c, to_z, to_d = to_c.astype(bf16), to_z.astype(bf16), to_d.astype(bf16)
    to_c, to_z, to_d, partial = lax.optimization_barrier((to_c, to_z, to_d, partial))
    from_z = lax.ppermute(to_z, "zl", SWAP)
    from_d = lax.ppermute(to_d, ("zl", "c"), ((0, 3), (1, 2), (2, 1), (3, 0)))
    from_c = lax.ppermute(to_c, "c", SWAP)
    scattered = lax.all_to_all(partial.reshape(64, 4, 2048), ("y", "x"), 0, 0)

    g_par = lax.ppermute(dot(kb_p, weights, 1, 0).astype(bf16), "zl", SWAP)
    grad_tokens = (dot(kb, weights, 1, 0) + g_par.astype(f32)).astype(bf16)

    near = keep + from_c.astype(f32)
    far = from_z.astype(f32) + from_d.astype(f32)
    total = jnp.where(zl == 0, jnp.concatenate([near, far], 1), jnp.concatenate([far, near], 1))
    total_b = total.astype(bf16)
    one, three, two = (
        lax.ppermute(total_b, "zh", [(i, (i + step) % 4) for i in range(4)]).astype(f32)
        for step in (1, 3, 2)
    )
    total = (total_b.astype(f32) + two) + (one + three)
    own_cos, own_sin = cut(cosine, mine), cut(sine, mine)
    keys = rotate(total, own_cos, own_sin, 1.0).astype(bf16)
    others = lax.ppermute(keys, "c", SWAP)
    keys = jnp.where(core == 0, jnp.concatenate([keys, others]), jnp.concatenate([others, keys]))

    grad_key_weight = jnp.sum(scattered.astype(f32), axis=0)
    return keys, grad_tokens, grad_key_weight


def solution(mesh):
    fine = Mesh(mesh.devices.reshape(2, 8, 8, 4, 2), ("zl", "y", "x", "zh", "c"))
    fsdp, tensor = ("zl", "y", "x"), ("zh", "c")
    placed = (P(fsdp, tensor), P(fsdp, None), P(fsdp, tensor), P(fsdp, None))
    return jax.shard_map(
        body,
        mesh=fine,
        in_specs=placed,
        out_specs=(P(fsdp, None), P(fsdp, tensor), P(fsdp, tensor)),
        check_vma=False,
    )
```

```python
import jax
import jax.numpy as jnp
from jax import lax
from jax.experimental import pallas as pl
from jax.experimental.pallas import tpu as pltpu
from jax.sharding import Mesh, PartitionSpec as P

HEAD = 128
SWAP = ((0, 1), (1, 0))


def doc_positions(segments):
    index = jnp.arange(segments.shape[0], dtype=jnp.int32)
    return index - jnp.sum((segments[None, :] < segments[:, None]).astype(jnp.int32), axis=1)


def angles(positions, half):
    freq = 500000.0 ** (-2.0 * jnp.arange(half, dtype=jnp.float32) / (2 * half))
    turn = positions.astype(jnp.float32)[:, None] * freq[None, :]
    return (jnp.cos(turn)[:, None, :], jnp.sin(turn)[:, None, :])


def rotate(field, cosine, sine, sign):
    rows = field.shape[0]
    shaped = field.reshape(rows, -1, HEAD)
    first, second = (shaped[..., : HEAD // 2], shaped[..., HEAD // 2 :])
    out = jnp.concatenate(
        [first * cosine - sign * second * sine, second * cosine + sign * first * sine], axis=-1
    )
    return out.reshape(rows, -1)


def dot(a, b, da, db):
    return lax.dot_general(a, b, (((da,), (db,)), ((), ())), preferred_element_type=jnp.float32)


def kraw_kernel(tok_ref, par_ref, w_ref, keep_ref, send_ref):
    mine = pl.multiple_of(lax.axis_index("c") * 64, 64)
    other = pl.multiple_of(64 - mine, 64)
    halves = [ref[pl.ds(at, 64), :] for at in (mine, other) for ref in (tok_ref, par_ref)]
    out = dot(jnp.concatenate(halves, axis=0), w_ref[...], 1, 1)
    keep_ref[...] = out[:128]
    send_ref[...] = out[128:].astype(jnp.bfloat16)


def merge_kernel(keep_ref, c_ref, own_ref, far_ref):
    out = (keep_ref[...] + c_ref[...].astype(jnp.float32)).astype(jnp.bfloat16)
    own_ref[...] = out[:64]
    far_ref[...] = out[64:]


def grad_kernel(kb_ref, w_ref, add_ref, out_ref):
    out = dot(kb_ref[...], w_ref[...], 1, 0) + add_ref[...].astype(jnp.float32)
    out_ref[...] = out.astype(jnp.bfloat16)


def whole(kernel, outs, n_in, name):
    vmem = pl.BlockSpec(memory_space=pltpu.VMEM)
    return pl.pallas_call(
        kernel,
        out_shape=outs,
        in_specs=[vmem] * n_in,
        out_specs=jax.tree.map(lambda _: vmem, outs),
        compiler_params=pltpu.CompilerParams(vmem_limit_bytes=32 << 20),
        name=name,
    )


def body(tokens, seg_ids, key_weight, key_grad):
    bf16, f32 = jnp.bfloat16, jnp.float32
    shape = jax.ShapeDtypeStruct
    zl, core = lax.axis_index("zl"), lax.axis_index("c")
    spread = jnp.broadcast_to(key_weight[None], (64, 4, 2048))
    gathered = lax.all_to_all(spread, ("y", "x"), 0, 0)
    tok_p = lax.ppermute(tokens, "zl", SWAP)

    cosine, sine = angles(doc_positions(seg_ids[0]), HEAD // 2)
    kback = rotate(key_grad.astype(f32), cosine, sine, -1.0).astype(bf16)
    left, right = kback[:, :256], kback[:, 256:]
    kb_p = lax.ppermute(jnp.where(zl == 0, right, left), "zl", SWAP)
    kb = jnp.where(zl == 0, left, right)

    partial = (dot(kb, tokens, 0, 0) + dot(kb_p, tok_p, 0, 0)).astype(bf16).reshape(64, 4, 2048)

    weights = gathered.reshape(256, 2048)
    keep, to_c = whole(kraw_kernel, (shape((128, 256), f32), shape((128, 256), bf16)), 3, "kraw")(
        tokens, tok_p, weights
    )
    g_send = dot(kb_p, weights, 1, 0).astype(bf16)
    to_c, partial = lax.optimization_barrier((to_c, partial))
    from_c = lax.ppermute(to_c, "c", SWAP)
    half = shape((64, 256), bf16)
    own, to_z = whole(merge_kernel, (half, half), 2, "merge")(keep, from_c)
    from_z = lax.ppermute(to_z, "zl", SWAP)
    g_par = lax.ppermute(g_send, "zl", SWAP)
    scattered = lax.all_to_all(partial, ("y", "x"), 0, 0)

    total_b = jnp.where(
        zl == 0, jnp.concatenate([own, from_z], 1), jnp.concatenate([from_z, own], 1)
    )
    one, three, two = (
        lax.ppermute(total_b, "zh", [(i, (i + step) % 4) for i in range(4)])
        for step in (1, 3, 2)
    )
    one, three, two, g_par = lax.optimization_barrier((one, three, two, g_par))
    total = (total_b.astype(f32) + two.astype(f32)) + (one.astype(f32) + three.astype(f32))
    own_cos = lax.dynamic_slice_in_dim(cosine, core * 64, 64, 0)
    own_sin = lax.dynamic_slice_in_dim(sine, core * 64, 64, 0)
    keys = rotate(total, own_cos, own_sin, 1.0).astype(bf16)
    others = lax.ppermute(keys, "c", SWAP)
    keys = jnp.where(core == 0, jnp.concatenate([keys, others]), jnp.concatenate([others, keys]))

    grad_tokens = whole(grad_kernel, shape((128, 2048), bf16), 3, "grad")(kb, weights, g_par)
    grad_key_weight = jnp.sum(scattered.astype(f32), axis=0)
    return keys, grad_tokens, grad_key_weight


def solution(mesh):
    fine = Mesh(mesh.devices.reshape(2, 8, 8, 4, 2), ("zl", "y", "x", "zh", "c"))
    fsdp, tensor = ("zl", "y", "x"), ("zh", "c")
    placed = (P(fsdp, tensor), P(fsdp, None), P(fsdp, tensor), P(fsdp, None))
    return jax.shard_map(
        body,
        mesh=fine,
        in_specs=placed,
        out_specs=(P(fsdp, None), P(fsdp, tensor), P(fsdp, tensor)),
        check_vma=False,
    )
```

```python
import jax
import jax.numpy as jnp
from jax import lax
from jax.experimental import pallas as pl
from jax.experimental.pallas import tpu as pltpu
from jax.sharding import Mesh, PartitionSpec as P

HEAD = 128
SWAP = ((0, 1), (1, 0))


def doc_positions(segments):
    index = jnp.arange(segments.shape[0], dtype=jnp.int32)
    return index - jnp.sum((segments[None, :] < segments[:, None]).astype(jnp.int32), axis=1)


def angles(positions, half):
    freq = 500000.0 ** (-2.0 * jnp.arange(half, dtype=jnp.float32) / (2 * half))
    turn = positions.astype(jnp.float32)[:, None] * freq[None, :]
    return (jnp.cos(turn)[:, None, :], jnp.sin(turn)[:, None, :])


def rotate(field, cosine, sine, sign):
    rows = field.shape[0]
    shaped = field.reshape(rows, -1, HEAD)
    first, second = (shaped[..., : HEAD // 2], shaped[..., HEAD // 2 :])
    out = jnp.concatenate(
        [first * cosine - sign * second * sine, second * cosine + sign * first * sine], axis=-1
    )
    return out.reshape(rows, -1)


def dot(a, b, da, db):
    return lax.dot_general(a, b, (((da,), (db,)), ((), ())), preferred_element_type=jnp.float32)


def spread_kernel(w_ref, out_ref):
    out_ref[...] = jnp.broadcast_to(w_ref[...][None], out_ref.shape)


def kraw_kernel(tok_ref, par_ref, w_ref, keep_ref, send_ref):
    mine = pl.multiple_of(lax.axis_index("c") * 64, 64)
    other = pl.multiple_of(64 - mine, 64)
    halves = [ref[pl.ds(at, 64), :] for at in (mine, other) for ref in (tok_ref, par_ref)]
    out = dot(jnp.concatenate(halves, axis=0), w_ref[...], 1, 1)
    keep_ref[...] = out[:128]
    send_ref[...] = out[128:].astype(jnp.bfloat16)


def merge_kernel(keep_ref, c_ref, own_ref, far_ref):
    out = (keep_ref[...] + c_ref[...].astype(jnp.float32)).astype(jnp.bfloat16)
    own_ref[...] = out[:64]
    far_ref[...] = out[64:]


def grad_kernel(kb_ref, w_ref, add_ref, out_ref):
    out = dot(kb_ref[...], w_ref[...], 1, 0) + add_ref[...].astype(jnp.float32)
    out_ref[...] = out.astype(jnp.bfloat16)


def whole(kernel, outs, n_in, name):
    vmem = pl.BlockSpec(memory_space=pltpu.VMEM)
    return pl.pallas_call(
        kernel,
        out_shape=outs,
        in_specs=[vmem] * n_in,
        out_specs=jax.tree.map(lambda _: vmem, outs),
        compiler_params=pltpu.CompilerParams(vmem_limit_bytes=32 << 20),
        name=name,
    )


def body(tokens, seg_ids, key_weight, key_grad):
    bf16, f32 = jnp.bfloat16, jnp.float32
    shape = jax.ShapeDtypeStruct
    zl, core = lax.axis_index("zl"), lax.axis_index("c")
    spread = whole(spread_kernel, shape((64, 4, 2048), bf16), 1, "spread")(key_weight)
    gathered = lax.all_to_all(spread, ("y", "x"), 0, 0)
    tok_p = lax.ppermute(tokens, "zl", SWAP)

    cosine, sine = angles(doc_positions(seg_ids[0]), HEAD // 2)
    kback = rotate(key_grad.astype(f32), cosine, sine, -1.0).astype(bf16)
    left, right = kback[:, :256], kback[:, 256:]
    kb_p = lax.ppermute(jnp.where(zl == 0, right, left), "zl", SWAP)
    kb = jnp.where(zl == 0, left, right)

    partial = (dot(kb, tokens, 0, 0) + dot(kb_p, tok_p, 0, 0)).astype(bf16).reshape(64, 4, 2048)

    weights = gathered.reshape(256, 2048)
    keep, to_c = whole(kraw_kernel, (shape((128, 256), f32), shape((128, 256), bf16)), 3, "kraw")(
        tokens, tok_p, weights
    )
    to_c, partial = lax.optimization_barrier((to_c, partial))
    from_c = lax.ppermute(to_c, "c", SWAP)
    half = shape((64, 256), bf16)
    own, to_z = whole(merge_kernel, (half, half), 2, "merge")(keep, from_c)
    from_z = lax.ppermute(to_z, "zl", SWAP)
    scattered = lax.all_to_all(partial, ("y", "x"), 0, 0)

    total_b = jnp.where(
        zl == 0, jnp.concatenate([own, from_z], 1), jnp.concatenate([from_z, own], 1)
    )
    total_b, kb_p = lax.optimization_barrier((total_b, kb_p))
    g_par = lax.ppermute(dot(kb_p, weights, 1, 0).astype(bf16), "zl", SWAP)
    one, three, two = (
        lax.ppermute(total_b, "zh", [(i, (i + step) % 4) for i in range(4)])
        for step in (1, 3, 2)
    )
    total = (total_b.astype(f32) + two.astype(f32)) + (one.astype(f32) + three.astype(f32))
    own_cos = lax.dynamic_slice_in_dim(cosine, core * 64, 64, 0)
    own_sin = lax.dynamic_slice_in_dim(sine, core * 64, 64, 0)
    keys = rotate(total, own_cos, own_sin, 1.0).astype(bf16)
    others = lax.ppermute(keys, "c", SWAP)
    keys = jnp.where(core == 0, jnp.concatenate([keys, others]), jnp.concatenate([others, keys]))

    grad_tokens = whole(grad_kernel, shape((128, 2048), bf16), 3, "grad")(kb, weights, g_par)
    grad_key_weight = jnp.sum(scattered.astype(f32), axis=0)
    return keys, grad_tokens, grad_key_weight


def solution(mesh):
    fine = Mesh(mesh.devices.reshape(2, 8, 8, 4, 2), ("zl", "y", "x", "zh", "c"))
    fsdp, tensor = ("zl", "y", "x"), ("zh", "c")
    placed = (P(fsdp, tensor), P(fsdp, None), P(fsdp, tensor), P(fsdp, None))
    return jax.shard_map(
        body,
        mesh=fine,
        in_specs=placed,
        out_specs=(P(fsdp, None), P(fsdp, tensor), P(fsdp, tensor)),
        check_vma=False,
    )
```

```python
import jax
import jax.numpy as jnp
from jax import lax
from jax.experimental import pallas as pl
from jax.experimental.pallas import tpu as pltpu
from jax.sharding import Mesh, PartitionSpec as P

HEAD = 128
SWAP = ((0, 1), (1, 0))


def doc_positions(segments):
    index = jnp.arange(segments.shape[0], dtype=jnp.int32)
    return index - jnp.sum((segments[None, :] < segments[:, None]).astype(jnp.int32), axis=1)


def angles(positions, half):
    freq = 500000.0 ** (-2.0 * jnp.arange(half, dtype=jnp.float32) / (2 * half))
    turn = positions.astype(jnp.float32)[:, None] * freq[None, :]
    return (jnp.cos(turn)[:, None, :], jnp.sin(turn)[:, None, :])


def rotate(field, cosine, sine, sign):
    rows = field.shape[0]
    shaped = field.reshape(rows, -1, HEAD)
    first, second = (shaped[..., : HEAD // 2], shaped[..., HEAD // 2 :])
    out = jnp.concatenate(
        [first * cosine - sign * second * sine, second * cosine + sign * first * sine], axis=-1
    )
    return out.reshape(rows, -1)


def dot(a, b, da, db):
    return lax.dot_general(a, b, (((da,), (db,)), ((), ())), preferred_element_type=jnp.float32)


def spread_kernel(w_ref, out_ref):
    out_ref[...] = jnp.broadcast_to(w_ref[...][None], out_ref.shape)


def kraw_kernel(tok_ref, par_ref, w_ref, keep_ref, send_ref):
    mine = pl.multiple_of(lax.axis_index("c") * 64, 64)
    other = pl.multiple_of(64 - mine, 64)
    halves = [ref[pl.ds(at, 64), :] for at in (mine, other) for ref in (tok_ref, par_ref)]
    out = dot(jnp.concatenate(halves, axis=0), w_ref[...], 1, 1)
    keep_ref[...] = out[:128]
    send_ref[...] = out[128:].astype(jnp.bfloat16)


def merge_kernel(keep_ref, c_ref, own_ref, far_ref):
    theirs = c_ref[1 - lax.axis_index("c")].astype(jnp.float32)
    out = (keep_ref[...] + theirs).astype(jnp.bfloat16)
    own_ref[...] = out[:64]
    far_ref[...] = out[64:]


def grad_kernel(kb_ref, w_ref, add_ref, out_ref):
    out = dot(kb_ref[...], w_ref[...], 1, 0) + add_ref[...].astype(jnp.float32)
    out_ref[...] = out.astype(jnp.bfloat16)


def whole(kernel, outs, n_in, name):
    vmem = pl.BlockSpec(memory_space=pltpu.VMEM)
    return pl.pallas_call(
        kernel,
        out_shape=outs,
        in_specs=[vmem] * n_in,
        out_specs=jax.tree.map(lambda _: vmem, outs),
        compiler_params=pltpu.CompilerParams(vmem_limit_bytes=32 << 20),
        name=name,
    )


def body(tokens, seg_ids, key_weight, key_grad):
    bf16, f32 = jnp.bfloat16, jnp.float32
    shape = jax.ShapeDtypeStruct
    zl, core = lax.axis_index("zl"), lax.axis_index("c")
    spread = whole(spread_kernel, shape((64, 4, 2048), bf16), 1, "spread")(key_weight)
    gathered = lax.all_to_all(spread, ("y", "x"), 0, 0)
    tok_p = lax.ppermute(tokens, "zl", SWAP)

    cosine, sine = angles(doc_positions(seg_ids[0]), HEAD // 2)
    kback = rotate(key_grad.astype(f32), cosine, sine, -1.0).astype(bf16)
    left, right = kback[:, :256], kback[:, 256:]
    kb_p = lax.ppermute(jnp.where(zl == 0, right, left), "zl", SWAP)
    kb = jnp.where(zl == 0, left, right)

    partial = (dot(kb, tokens, 0, 0) + dot(kb_p, tok_p, 0, 0)).astype(bf16).reshape(64, 4, 2048)

    weights = gathered.reshape(256, 2048)
    keep, to_c = whole(kraw_kernel, (shape((128, 256), f32), shape((128, 256), bf16)), 3, "kraw")(
        tokens, tok_p, weights
    )
    to_c, partial = lax.optimization_barrier((to_c, partial))
    from_c = lax.all_gather(to_c, "c")
    half = shape((64, 256), bf16)
    own, to_z = whole(merge_kernel, (half, half), 2, "merge")(keep, from_c)
    from_z = lax.all_gather(to_z, "zl")
    scattered = lax.all_to_all(partial, ("y", "x"), 0, 0)

    total_b = jnp.where(
        zl == 0, jnp.concatenate([own, from_z[1]], 1), jnp.concatenate([from_z[0], own], 1)
    )
    total_b, kb_p = lax.optimization_barrier((total_b, kb_p))
    g_par = lax.ppermute(dot(kb_p, weights, 1, 0).astype(bf16), "zl", SWAP)
    every = lax.all_gather(total_b, "zh")
    every, g_par = lax.optimization_barrier((every, g_par))
    total = jnp.sum(every.astype(f32), axis=0)
    own_cos = lax.dynamic_slice_in_dim(cosine, core * 64, 64, 0)
    own_sin = lax.dynamic_slice_in_dim(sine, core * 64, 64, 0)
    keys = rotate(total, own_cos, own_sin, 1.0).astype(bf16)
    keys = lax.all_gather(keys, "c", axis=0, tiled=True)

    grad_tokens = whole(grad_kernel, shape((128, 2048), bf16), 3, "grad")(kb, weights, g_par)
    grad_key_weight = jnp.sum(scattered.astype(f32), axis=0)
    return keys, grad_tokens, grad_key_weight


def solution(mesh):
    fine = Mesh(mesh.devices.reshape(2, 8, 8, 4, 2), ("zl", "y", "x", "zh", "c"))
    fsdp, tensor = ("zl", "y", "x"), ("zh", "c")
    placed = (P(fsdp, tensor), P(fsdp, None), P(fsdp, tensor), P(fsdp, None))
    return jax.shard_map(
        body,
        mesh=fine,
        in_specs=placed,
        out_specs=(P(fsdp, None), P(fsdp, tensor), P(fsdp, tensor)),
        check_vma=False,
    )
```

```python
import jax
import jax.numpy as jnp
from jax import lax
from jax.experimental import pallas as pl
from jax.experimental.pallas import tpu as pltpu
from jax.sharding import Mesh, PartitionSpec as P

HEAD = 128
SWAP = ((0, 1), (1, 0))


def doc_positions(segments):
    index = jnp.arange(segments.shape[0], dtype=jnp.int32)
    return index - jnp.sum((segments[None, :] < segments[:, None]).astype(jnp.int32), axis=1)


def angles(positions, half):
    freq = 500000.0 ** (-2.0 * jnp.arange(half, dtype=jnp.float32) / (2 * half))
    turn = positions.astype(jnp.float32)[:, None] * freq[None, :]
    return (jnp.cos(turn)[:, None, :], jnp.sin(turn)[:, None, :])


def rotate(field, cosine, sine, sign):
    rows = field.shape[0]
    shaped = field.reshape(rows, -1, HEAD)
    first, second = (shaped[..., : HEAD // 2], shaped[..., HEAD // 2 :])
    out = jnp.concatenate(
        [first * cosine - sign * second * sine, second * cosine + sign * first * sine], axis=-1
    )
    return out.reshape(rows, -1)


def dot(a, b, da, db):
    return lax.dot_general(a, b, (((da,), (db,)), ((), ())), preferred_element_type=jnp.float32)


def ahead(k):
    pairs = []
    for y in range(8):
        for x in range(8):
            pairs.append(((y * 8 + x) * 2, ((y + k) % 8 * 8 + x) * 2))
            pairs.append(((y * 8 + x) * 2 + 1, (y * 8 + (x + k) % 8) * 2 + 1))
    return pairs


def across():
    rows = [[(y * 8 + x) * 2 for x in range(8)] for y in range(8)]
    return rows + [[(y * 8 + x) * 2 + 1 for y in range(8)] for x in range(8)]


def spread_kernel(w_ref, out_ref):
    out_ref[...] = jnp.broadcast_to(w_ref[...][None], out_ref.shape)


def partial_kernel(kb_ref, kbp_ref, tok_ref, par_ref, own_ref, *out_refs):
    bf16 = jnp.bfloat16
    core = lax.axis_index("c")
    place = jnp.where(core == 0, lax.axis_index("y"), lax.axis_index("x"))
    row = lax.broadcasted_iota(jnp.int32, (256, 256), 0)
    feature = lax.broadcasted_iota(jnp.int32, (256, 256), 1)
    ahead, inner = ((row >> 5) + place) & 7, row & 31
    by_y = ahead * 32 + inner
    by_x = (inner >> 2) * 32 + ahead * 4 + (inner & 3)
    pick = jnp.where(feature == jnp.where(core == 0, by_y, by_x), 1.0, 0.0).astype(bf16)
    out = dot(dot(pick, kb_ref[...], 1, 1).astype(bf16), tok_ref[...], 1, 0)
    out = out + dot(dot(pick, kbp_ref[...], 1, 1).astype(bf16), par_ref[...], 1, 0)
    own_ref[...] = out[:32]
    for k, out_ref in enumerate(out_refs):
        out_ref[...] = out[32 * (k + 1) : 32 * (k + 2)].astype(bf16)


def total_kernel(own_ref, *refs):
    total = own_ref[...]
    for ref in refs[:-1]:
        total = total + ref[...].astype(jnp.float32)
    refs[-1][...] = total.astype(jnp.bfloat16)


def kraw_kernel(tok_ref, par_ref, w_ref, out_ref):
    at = lax.axis_index("zl") * 128
    own, far = pl.multiple_of(at, 128), pl.multiple_of(128 - at, 128)
    both = jnp.concatenate([tok_ref[...], par_ref[...]], axis=0)
    out = dot(both, w_ref[...], 1, 1).astype(jnp.bfloat16)
    out_ref[pl.ds(own, 128), :] = out[:128]
    out_ref[pl.ds(far, 128), :] = out[128:]


def grad_kernel(kb_ref, w_ref, add_ref, out_ref):
    out = dot(kb_ref[...], w_ref[...], 1, 0) + add_ref[...].astype(jnp.float32)
    out_ref[...] = out.astype(jnp.bfloat16)


def whole(kernel, outs, n_in, name):
    vmem = pl.BlockSpec(memory_space=pltpu.VMEM)
    return pl.pallas_call(
        kernel,
        out_shape=outs,
        in_specs=[vmem] * n_in,
        out_specs=jax.tree.map(lambda _: vmem, outs),
        compiler_params=pltpu.CompilerParams(vmem_limit_bytes=32 << 20),
        name=name,
    )


def body(tokens, seg_ids, key_weight, key_grad):
    bf16, f32 = jnp.bfloat16, jnp.float32
    shape = jax.ShapeDtypeStruct
    zl, t = lax.axis_index("zl"), lax.axis_index("zh") * 2 + lax.axis_index("c")
    spread = whole(spread_kernel, shape((64, 4, 2048), bf16), 1, "spread")(key_weight)
    gathered = lax.all_to_all(spread, ("y", "x"), 0, 0)
    tok_p = lax.ppermute(tokens, "zl", SWAP)

    cosine, sine = angles(doc_positions(seg_ids[0]), HEAD // 2)
    kback = rotate(key_grad.astype(f32), cosine, sine, -1.0).astype(bf16)
    left, right = kback[:, :256], kback[:, 256:]
    kb_p = lax.ppermute(jnp.where(zl == 0, right, left), "zl", SWAP)
    kb = jnp.where(zl == 0, left, right)

    part = shape((32, 2048), bf16)
    own, *parts = whole(
        partial_kernel, (shape((32, 2048), f32),) + (part,) * 7, 4, "partial"
    )(kb, kb_p, tokens, tok_p)
    arrived = [
        lax.ppermute(parts[k - 1], ("y", "x", "c"), ahead(k)) for k in range(1, 8)
    ]
    summed = whole(total_kernel, part, 8, "total")(own, *arrived)

    gathered, summed = lax.optimization_barrier((gathered, summed))
    weights = gathered.reshape(256, 2048)
    ks = whole(kraw_kernel, shape((256, 256), bf16), 3, "kraw")(tokens, tok_p, weights)
    ks = lax.all_to_all(ks.reshape(16, 16, 256), ("zl", "zh", "c"), 0, 0)
    g_par = lax.ppermute(dot(kb_p, weights, 1, 0).astype(bf16), "zl", SWAP)
    ks, summed, g_par = lax.optimization_barrier((ks, summed, g_par))
    scattered = lax.all_to_all(
        summed.reshape(8, 4, 2048), ("y", "x", "c"), 0, 0, axis_index_groups=across()
    )
    total = jnp.sum(ks.reshape(2, 8, 16, 256).astype(f32), axis=1)
    total = total.transpose(1, 0, 2).reshape(16, 512)
    own_cos = lax.dynamic_slice_in_dim(cosine, t * 16, 16, 0)
    own_sin = lax.dynamic_slice_in_dim(sine, t * 16, 16, 0)
    keys = rotate(total, own_cos, own_sin, 1.0).astype(bf16)
    keys = lax.all_gather(lax.all_gather(keys, "c", axis=0, tiled=True), "zh", axis=0, tiled=True)

    grad_tokens = whole(grad_kernel, shape((128, 2048), bf16), 3, "grad")(kb, weights, g_par)
    grad_key_weight = jnp.sum(scattered.astype(f32), axis=0)
    return keys, grad_tokens, grad_key_weight


def solution(mesh):
    fine = Mesh(mesh.devices.reshape(2, 8, 8, 4, 2), ("zl", "y", "x", "zh", "c"))
    fsdp, tensor = ("zl", "y", "x"), ("zh", "c")
    placed = (P(fsdp, tensor), P(fsdp, None), P(fsdp, tensor), P(fsdp, None))
    return jax.shard_map(
        body,
        mesh=fine,
        in_specs=placed,
        out_specs=(P(fsdp, None), P(fsdp, tensor), P(fsdp, tensor)),
        check_vma=False,
    )
```

```python
import jax
import jax.numpy as jnp
from jax import lax
from jax.experimental import pallas as pl
from jax.experimental.pallas import tpu as pltpu
from jax.sharding import Mesh, PartitionSpec as P

HEAD = 128
SWAP = ((0, 1), (1, 0))


def doc_positions(segments):
    index = jnp.arange(segments.shape[0], dtype=jnp.int32)
    return index - jnp.sum((segments[None, :] < segments[:, None]).astype(jnp.int32), axis=1)


def angles(positions, half):
    freq = 500000.0 ** (-2.0 * jnp.arange(half, dtype=jnp.float32) / (2 * half))
    turn = positions.astype(jnp.float32)[:, None] * freq[None, :]
    return (jnp.cos(turn)[:, None, :], jnp.sin(turn)[:, None, :])


def rotate(field, cosine, sine, sign):
    rows = field.shape[0]
    shaped = field.reshape(rows, -1, HEAD)
    first, second = (shaped[..., : HEAD // 2], shaped[..., HEAD // 2 :])
    out = jnp.concatenate(
        [first * cosine - sign * second * sine, second * cosine + sign * first * sine], axis=-1
    )
    return out.reshape(rows, -1)


def dot(a, b, da, db):
    return lax.dot_general(a, b, (((da,), (db,)), ((), ())), preferred_element_type=jnp.float32)


def spread_kernel(w_ref, out_ref):
    out_ref[...] = jnp.broadcast_to(w_ref[...][None], out_ref.shape)


def kraw_kernel(tok_ref, par_ref, kb_ref, w_ref, keep_ref, send_ref, grad_ref):
    mine = pl.multiple_of(lax.axis_index("c") * 64, 64)
    other = pl.multiple_of(64 - mine, 64)
    halves = [ref[pl.ds(at, 64), :] for at in (mine, other) for ref in (tok_ref, par_ref)]
    out = dot(jnp.concatenate(halves, axis=0), w_ref[...], 1, 1)
    keep_ref[...] = out[:128]
    send_ref[...] = out[128:].astype(jnp.bfloat16)
    grad_ref[...] = dot(kb_ref[...], w_ref[...], 1, 0).astype(jnp.bfloat16)


def merge_kernel(keep_ref, c_ref, own_ref, far_ref):
    theirs = c_ref[1 - lax.axis_index("c")].astype(jnp.float32)
    out = (keep_ref[...] + theirs).astype(jnp.bfloat16)
    own_ref[...] = out[:64]
    far_ref[...] = out[64:]


def grad_kernel(kb_ref, w_ref, add_ref, out_ref):
    out = dot(kb_ref[...], w_ref[...], 1, 0) + add_ref[...].astype(jnp.float32)
    out_ref[...] = out.astype(jnp.bfloat16)


def whole(kernel, outs, n_in, name):
    vmem = pl.BlockSpec(memory_space=pltpu.VMEM)
    return pl.pallas_call(
        kernel,
        out_shape=outs,
        in_specs=[vmem] * n_in,
        out_specs=jax.tree.map(lambda _: vmem, outs),
        compiler_params=pltpu.CompilerParams(vmem_limit_bytes=32 << 20),
        name=name,
    )


def body(tokens, seg_ids, key_weight, key_grad):
    bf16, f32 = jnp.bfloat16, jnp.float32
    shape = jax.ShapeDtypeStruct
    zl, core = lax.axis_index("zl"), lax.axis_index("c")
    spread = whole(spread_kernel, shape((64, 4, 2048), bf16), 1, "spread")(key_weight)
    gathered = lax.all_to_all(spread, ("y", "x"), 0, 0)
    tok_p = lax.ppermute(tokens, "zl", SWAP)

    cosine, sine = angles(doc_positions(seg_ids[0]), HEAD // 2)
    kback = rotate(key_grad.astype(f32), cosine, sine, -1.0).astype(bf16)
    left, right = kback[:, :256], kback[:, 256:]
    kb_p = lax.ppermute(jnp.where(zl == 0, right, left), "zl", SWAP)
    kb = jnp.where(zl == 0, left, right)

    partial = (dot(kb, tokens, 0, 0) + dot(kb_p, tok_p, 0, 0)).astype(bf16).reshape(64, 4, 2048)

    weights = gathered.reshape(256, 2048)
    keep, to_c, g_send = whole(
        kraw_kernel,
        (shape((128, 256), f32), shape((128, 256), bf16), shape((128, 2048), bf16)),
        4,
        "kraw",
    )(tokens, tok_p, kb_p, weights)
    g_par = lax.ppermute(g_send, "zl", SWAP)
    to_c, partial = lax.optimization_barrier((to_c, partial))
    from_c = lax.all_gather(to_c, "c")
    half = shape((64, 256), bf16)
    own, to_z = whole(merge_kernel, (half, half), 2, "merge")(keep, from_c)
    from_z = lax.all_gather(to_z, "zl")
    scattered = lax.all_to_all(partial, ("y", "x"), 0, 0)

    total_b = jnp.where(
        zl == 0, jnp.concatenate([own, from_z[1]], 1), jnp.concatenate([from_z[0], own], 1)
    )
    one, three, two = (
        lax.ppermute(total_b, "zh", [(i, (i + step) % 4) for i in range(4)])
        for step in (1, 3, 2)
    )
    total = (total_b.astype(f32) + two.astype(f32)) + (one.astype(f32) + three.astype(f32))
    own_cos = lax.dynamic_slice_in_dim(cosine, core * 64, 64, 0)
    own_sin = lax.dynamic_slice_in_dim(sine, core * 64, 64, 0)
    keys = rotate(total, own_cos, own_sin, 1.0).astype(bf16)
    keys = lax.all_gather(keys, "c", axis=0, tiled=True)

    grad_key_weight = jnp.sum(scattered.astype(f32), axis=0)
    grad_key_weight, g_par = lax.optimization_barrier((grad_key_weight, g_par))
    grad_tokens = whole(grad_kernel, shape((128, 2048), bf16), 3, "grad")(kb, weights, g_par)
    return keys, grad_tokens, grad_key_weight


def solution(mesh):
    fine = Mesh(mesh.devices.reshape(2, 8, 8, 4, 2), ("zl", "y", "x", "zh", "c"))
    fsdp, tensor = ("zl", "y", "x"), ("zh", "c")
    placed = (P(fsdp, tensor), P(fsdp, None), P(fsdp, tensor), P(fsdp, None))
    return jax.shard_map(
        body,
        mesh=fine,
        in_specs=placed,
        out_specs=(P(fsdp, None), P(fsdp, tensor), P(fsdp, tensor)),
        check_vma=False,
    )
```

```python
import jax
import jax.numpy as jnp
from jax import lax
from jax.experimental import pallas as pl
from jax.experimental.pallas import tpu as pltpu
from jax.sharding import Mesh, PartitionSpec as P

HEAD = 128
SWAP = ((0, 1), (1, 0))


def doc_positions(segments):
    index = jnp.arange(segments.shape[0], dtype=jnp.int32)
    return index - jnp.sum((segments[None, :] < segments[:, None]).astype(jnp.int32), axis=1)


def angles(positions, half):
    freq = 500000.0 ** (-2.0 * jnp.arange(half, dtype=jnp.float32) / (2 * half))
    turn = positions.astype(jnp.float32)[:, None] * freq[None, :]
    return (jnp.cos(turn)[:, None, :], jnp.sin(turn)[:, None, :])


def rotate(field, cosine, sine, sign):
    rows = field.shape[0]
    shaped = field.reshape(rows, -1, HEAD)
    first, second = (shaped[..., : HEAD // 2], shaped[..., HEAD // 2 :])
    out = jnp.concatenate(
        [first * cosine - sign * second * sine, second * cosine + sign * first * sine], axis=-1
    )
    return out.reshape(rows, -1)


def dot(a, b, da, db):
    return lax.dot_general(a, b, (((da,), (db,)), ((), ())), preferred_element_type=jnp.float32)


def spread_kernel(w_ref, out_ref):
    out_ref[...] = jnp.broadcast_to(w_ref[...][None], out_ref.shape)


def kraw_kernel(tok_ref, par_ref, kb_ref, w_ref, keep_ref, send_ref, grad_ref):
    mine = pl.multiple_of(lax.axis_index("c") * 64, 64)
    other = pl.multiple_of(64 - mine, 64)
    halves = [ref[pl.ds(at, 64), :] for at in (mine, other) for ref in (tok_ref, par_ref)]
    out = dot(jnp.concatenate(halves, axis=0), w_ref[...], 1, 1)
    keep_ref[...] = out[:128]
    send_ref[...] = out[128:].astype(jnp.bfloat16)
    grad_ref[...] = dot(kb_ref[...], w_ref[...], 1, 0).astype(jnp.bfloat16)


def merge_kernel(keep_ref, c_ref, own_ref, far_ref):
    theirs = c_ref[1 - lax.axis_index("c")].astype(jnp.float32)
    out = (keep_ref[...] + theirs).astype(jnp.bfloat16)
    own_ref[...] = out[:64]
    far_ref[...] = out[64:]


def grad_kernel(kb_ref, w_ref, add_ref, out_ref):
    out = dot(kb_ref[...], w_ref[...], 1, 0) + add_ref[...].astype(jnp.float32)
    out_ref[...] = out.astype(jnp.bfloat16)


def sum_kernel(in_ref, out_ref):
    out_ref[...] = jnp.sum(in_ref[...].astype(jnp.float32), axis=0)


def whole(kernel, outs, n_in, name):
    vmem = pl.BlockSpec(memory_space=pltpu.VMEM)
    return pl.pallas_call(
        kernel,
        out_shape=outs,
        in_specs=[vmem] * n_in,
        out_specs=jax.tree.map(lambda _: vmem, outs),
        compiler_params=pltpu.CompilerParams(vmem_limit_bytes=12 << 20),
        name=name,
    )


def body(tokens, seg_ids, key_weight, key_grad):
    bf16, f32 = jnp.bfloat16, jnp.float32
    shape = jax.ShapeDtypeStruct
    zl, core = lax.axis_index("zl"), lax.axis_index("c")
    spread = whole(spread_kernel, shape((64, 4, 2048), bf16), 1, "spread")(key_weight)
    gathered = lax.all_to_all(spread, ("y", "x"), 0, 0)
    tok_p = lax.ppermute(tokens, "zl", SWAP)

    cosine, sine = angles(doc_positions(seg_ids[0]), HEAD // 2)
    kback = rotate(key_grad.astype(f32), cosine, sine, -1.0).astype(bf16)
    left, right = kback[:, :256], kback[:, 256:]
    kb_p = lax.ppermute(jnp.where(zl == 0, right, left), "zl", SWAP)
    kb = jnp.where(zl == 0, left, right)

    partial = (dot(kb, tokens, 0, 0) + dot(kb_p, tok_p, 0, 0)).astype(bf16).reshape(64, 4, 2048)

    weights = gathered.reshape(256, 2048)
    keep, to_c, g_send = whole(
        kraw_kernel,
        (shape((128, 256), f32), shape((128, 256), bf16), shape((128, 2048), bf16)),
        4,
        "kraw",
    )(tokens, tok_p, kb_p, weights)
    g_par = lax.ppermute(g_send, "zl", SWAP)
    from_c = lax.all_gather(to_c, "c")
    half = shape((64, 256), bf16)
    own, to_z = whole(merge_kernel, (half, half), 2, "merge")(keep, from_c)
    from_z = lax.all_gather(to_z, "zl")
    scattered = lax.all_to_all(partial, ("y", "x"), 0, 0)

    total_b = jnp.where(
        zl == 0, jnp.concatenate([own, from_z[1]], 1), jnp.concatenate([from_z[0], own], 1)
    )
    one, three, two = (
        lax.ppermute(total_b, "zh", [(i, (i + step) % 4) for i in range(4)])
        for step in (1, 3, 2)
    )
    total = (total_b.astype(f32) + two.astype(f32)) + (one.astype(f32) + three.astype(f32))
    own_cos = lax.dynamic_slice_in_dim(cosine, core * 64, 64, 0)
    own_sin = lax.dynamic_slice_in_dim(sine, core * 64, 64, 0)
    keys = rotate(total, own_cos, own_sin, 1.0).astype(bf16)
    keys = lax.all_gather(keys, "c", axis=0, tiled=True)

    grad_key_weight = whole(sum_kernel, shape((4, 2048), f32), 1, "sum")(scattered)
    grad_key_weight, g_par = lax.optimization_barrier((grad_key_weight, g_par))
    grad_tokens = whole(grad_kernel, shape((128, 2048), bf16), 3, "grad")(kb, weights, g_par)
    return keys, grad_tokens, grad_key_weight


def solution(mesh):
    fine = Mesh(mesh.devices.reshape(2, 8, 8, 4, 2), ("zl", "y", "x", "zh", "c"))
    fsdp, tensor = ("zl", "y", "x"), ("zh", "c")
    placed = (P(fsdp, tensor), P(fsdp, None), P(fsdp, tensor), P(fsdp, None))
    return jax.shard_map(
        body,
        mesh=fine,
        in_specs=placed,
        out_specs=(P(fsdp, None), P(fsdp, tensor), P(fsdp, tensor)),
        check_vma=False,
    )
```

```python
import jax
import jax.numpy as jnp
from jax import lax
from jax.experimental import pallas as pl
from jax.experimental.pallas import tpu as pltpu
from jax.sharding import Mesh, PartitionSpec as P

HEAD = 128
SWAP = ((0, 1), (1, 0))


def doc_positions(segments):
    index = jnp.arange(segments.shape[0], dtype=jnp.int32)
    return index - jnp.sum((segments[None, :] < segments[:, None]).astype(jnp.int32), axis=1)


def angles(positions, half):
    freq = 500000.0 ** (-2.0 * jnp.arange(half, dtype=jnp.float32) / (2 * half))
    turn = positions.astype(jnp.float32)[:, None] * freq[None, :]
    return (jnp.cos(turn)[:, None, :], jnp.sin(turn)[:, None, :])


def rotate(field, cosine, sine, sign):
    rows = field.shape[0]
    shaped = field.reshape(rows, -1, HEAD)
    first, second = (shaped[..., : HEAD // 2], shaped[..., HEAD // 2 :])
    out = jnp.concatenate(
        [first * cosine - sign * second * sine, second * cosine + sign * first * sine], axis=-1
    )
    return out.reshape(rows, -1)


def dot(a, b, da, db):
    return lax.dot_general(a, b, (((da,), (db,)), ((), ())), preferred_element_type=jnp.float32)


def spread_kernel(w_ref, out_ref):
    out_ref[...] = jnp.broadcast_to(w_ref[...][None], out_ref.shape)


def kraw_kernel(tok_ref, par_ref, kb_ref, w_ref, keep_ref, send_ref, grad_ref):
    mine = pl.multiple_of(lax.axis_index("c") * 64, 64)
    other = pl.multiple_of(64 - mine, 64)
    halves = [ref[pl.ds(at, 64), :] for at in (mine, other) for ref in (tok_ref, par_ref)]
    out = dot(jnp.concatenate(halves, axis=0), w_ref[...], 1, 1)
    keep_ref[...] = out[:128]
    send_ref[...] = out[128:].astype(jnp.bfloat16)
    grad_ref[...] = dot(kb_ref[...], w_ref[...], 1, 0).astype(jnp.bfloat16)


def merge_kernel(keep_ref, c_ref, own_ref, far_ref):
    theirs = c_ref[1 - lax.axis_index("c")].astype(jnp.float32)
    out = (keep_ref[...] + theirs).astype(jnp.bfloat16)
    own_ref[...] = out[:64]
    far_ref[...] = out[64:]


def grad_kernel(kb_ref, w_ref, add_ref, out_ref):
    out = dot(kb_ref[...], w_ref[...], 1, 0) + add_ref[...].astype(jnp.float32)
    out_ref[...] = out.astype(jnp.bfloat16)


def whole(kernel, outs, n_in, name):
    vmem = pl.BlockSpec(memory_space=pltpu.VMEM)
    return pl.pallas_call(
        kernel,
        out_shape=outs,
        in_specs=[vmem] * n_in,
        out_specs=jax.tree.map(lambda _: vmem, outs),
        compiler_params=pltpu.CompilerParams(vmem_limit_bytes=12 << 20),
        name=name,
    )


def body(tokens, seg_ids, key_weight, key_grad):
    bf16, f32 = jnp.bfloat16, jnp.float32
    shape = jax.ShapeDtypeStruct
    zl, core = lax.axis_index("zl"), lax.axis_index("c")
    spread = whole(spread_kernel, shape((64, 4, 2048), bf16), 1, "spread")(key_weight)
    gathered = lax.all_to_all(spread, ("y", "x"), 0, 0)
    tok_p = lax.ppermute(tokens, "zl", SWAP)

    cosine, sine = angles(doc_positions(seg_ids[0]), HEAD // 2)
    kback = rotate(key_grad.astype(f32), cosine, sine, -1.0).astype(bf16)
    left, right = kback[:, :256], kback[:, 256:]
    kb_p = lax.ppermute(jnp.where(zl == 0, right, left), "zl", SWAP)
    kb = jnp.where(zl == 0, left, right)

    partial = (dot(kb, tokens, 0, 0) + dot(kb_p, tok_p, 0, 0)).astype(bf16).reshape(64, 4, 2048)

    weights = gathered.reshape(256, 2048)
    keep, to_c, g_send = whole(
        kraw_kernel,
        (shape((128, 256), f32), shape((128, 256), bf16), shape((128, 2048), bf16)),
        4,
        "kraw",
    )(tokens, tok_p, kb_p, weights)
    g_par = lax.ppermute(g_send, "zl", SWAP)
    from_c = lax.all_gather(to_c, "c")
    half = shape((64, 256), bf16)
    own, to_z = whole(merge_kernel, (half, half), 2, "merge")(keep, from_c)
    from_z = lax.all_gather(to_z, "zl")
    scattered = lax.all_to_all(partial, ("y", "x"), 0, 0)

    total_b = jnp.where(
        zl == 0, jnp.concatenate([own, from_z[1]], 1), jnp.concatenate([from_z[0], own], 1)
    )
    one, three, two = (
        lax.ppermute(total_b, "zh", [(i, (i + step) % 4) for i in range(4)])
        for step in (1, 3, 2)
    )
    total = (three.astype(f32) + one.astype(f32)) + (two.astype(f32) + total_b.astype(f32))
    own_cos = lax.dynamic_slice_in_dim(cosine, core * 64, 64, 0)
    own_sin = lax.dynamic_slice_in_dim(sine, core * 64, 64, 0)
    keys = rotate(total, own_cos, own_sin, 1.0).astype(bf16)
    keys = lax.all_gather(keys, "c", axis=0, tiled=True)

    grad_key_weight = jnp.sum(scattered.astype(f32), axis=0)
    grad_key_weight, g_par = lax.optimization_barrier((grad_key_weight, g_par))
    grad_tokens = whole(grad_kernel, shape((128, 2048), bf16), 3, "grad")(kb, weights, g_par)
    return keys, grad_tokens, grad_key_weight


def solution(mesh):
    fine = Mesh(mesh.devices.reshape(2, 8, 8, 4, 2), ("zl", "y", "x", "zh", "c"))
    fsdp, tensor = ("zl", "y", "x"), ("zh", "c")
    placed = (P(fsdp, tensor), P(fsdp, None), P(fsdp, tensor), P(fsdp, None))
    return jax.shard_map(
        body,
        mesh=fine,
        in_specs=placed,
        out_specs=(P(fsdp, None), P(fsdp, tensor), P(fsdp, tensor)),
        check_vma=False,
    )
```

```python
import jax
import jax.numpy as jnp
from jax import lax
from jax.experimental import pallas as pl
from jax.experimental.pallas import tpu as pltpu
from jax.sharding import Mesh, PartitionSpec as P

HEAD = 128
SWAP = ((0, 1), (1, 0))


def doc_positions(segments):
    index = jnp.arange(segments.shape[0], dtype=jnp.int32)
    return index - jnp.sum((segments[None, :] < segments[:, None]).astype(jnp.int32), axis=1)


def angles(positions, half):
    freq = 500000.0 ** (-2.0 * jnp.arange(half, dtype=jnp.float32) / (2 * half))
    turn = positions.astype(jnp.float32)[:, None] * freq[None, :]
    return (jnp.cos(turn)[:, None, :], jnp.sin(turn)[:, None, :])


def rotate(field, cosine, sine, sign):
    rows = field.shape[0]
    shaped = field.reshape(rows, -1, HEAD)
    first, second = (shaped[..., : HEAD // 2], shaped[..., HEAD // 2 :])
    out = jnp.concatenate(
        [first * cosine - sign * second * sine, second * cosine + sign * first * sine], axis=-1
    )
    return out.reshape(rows, -1)


def dot(a, b, da, db):
    return lax.dot_general(a, b, (((da,), (db,)), ((), ())), preferred_element_type=jnp.float32)


def spread_kernel(w_ref, out_ref):
    out_ref[...] = jnp.broadcast_to(w_ref[...][None], out_ref.shape)


def kraw_kernel(tok_ref, par_ref, kb_ref, w_ref, keep_ref, send_ref, grad_ref):
    mine = pl.multiple_of(lax.axis_index("c") * 64, 64)
    other = pl.multiple_of(64 - mine, 64)
    halves = [ref[pl.ds(at, 64), :] for at in (mine, other) for ref in (tok_ref, par_ref)]
    out = dot(jnp.concatenate(halves, axis=0), w_ref[...], 1, 1)
    keep_ref[...] = out[:128]
    send_ref[...] = out[128:].astype(jnp.bfloat16)
    grad_ref[...] = dot(kb_ref[...], w_ref[...], 1, 0).astype(jnp.bfloat16)


def merge_kernel(keep_ref, c_ref, own_ref, far_ref):
    theirs = c_ref[1 - lax.axis_index("c")].astype(jnp.float32)
    out = (keep_ref[...] + theirs).astype(jnp.bfloat16)
    own_ref[...] = out[:64]
    far_ref[...] = out[64:]


def grad_kernel(kb_ref, w_ref, add_ref, out_ref):
    out = dot(kb_ref[...], w_ref[...], 1, 0) + add_ref[...].astype(jnp.float32)
    out_ref[...] = out.astype(jnp.bfloat16)


def whole(kernel, outs, n_in, name):
    vmem = pl.BlockSpec(memory_space=pltpu.VMEM)
    return pl.pallas_call(
        kernel,
        out_shape=outs,
        in_specs=[vmem] * n_in,
        out_specs=jax.tree.map(lambda _: vmem, outs),
        compiler_params=pltpu.CompilerParams(vmem_limit_bytes=12 << 20),
        name=name,
    )


def body(tokens, seg_ids, key_weight, key_grad):
    bf16, f32 = jnp.bfloat16, jnp.float32
    shape = jax.ShapeDtypeStruct
    zl, core = lax.axis_index("zl"), lax.axis_index("c")
    spread = whole(spread_kernel, shape((64, 4, 2048), bf16), 1, "spread")(key_weight)
    gathered = lax.all_to_all(spread, ("y", "x"), 0, 0)
    tok_p = lax.ppermute(tokens, "zl", SWAP)

    cosine, sine = angles(doc_positions(seg_ids[0]), HEAD // 2)
    kback = rotate(key_grad.astype(f32), cosine, sine, -1.0).astype(bf16)
    left, right = kback[:, :256], kback[:, 256:]
    kb_p = lax.ppermute(jnp.where(zl == 0, right, left), "zl", SWAP)
    kb = jnp.where(zl == 0, left, right)

    partial = (dot(kb, tokens, 0, 0) + dot(kb_p, tok_p, 0, 0)).astype(bf16).reshape(64, 4, 2048)

    weights = gathered.reshape(256, 2048)
    keep, to_c, g_send = whole(
        kraw_kernel,
        (shape((128, 256), f32), shape((128, 256), bf16), shape((128, 2048), bf16)),
        4,
        "kraw",
    )(tokens, tok_p, kb_p, weights)
    from_c = lax.all_gather(to_c, "c")
    half = shape((64, 256), bf16)
    own, to_z = whole(merge_kernel, (half, half), 2, "merge")(keep, from_c)
    from_z = lax.all_gather(to_z, "zl")
    scattered = lax.all_to_all(partial, ("y", "x"), 0, 0)

    total_b = jnp.where(
        zl == 0, jnp.concatenate([own, from_z[1]], 1), jnp.concatenate([from_z[0], own], 1)
    )
    total_b, g_send = lax.optimization_barrier((total_b, g_send))
    g_par = lax.ppermute(g_send, "zl", SWAP)
    one, three, two = (
        lax.ppermute(total_b, "zh", [(i, (i + step) % 4) for i in range(4)])
        for step in (1, 3, 2)
    )
    grad_tokens = whole(grad_kernel, shape((128, 2048), bf16), 3, "grad")(kb, weights, g_par)
    three, one, two, grad_tokens = lax.optimization_barrier((three, one, two, grad_tokens))
    total = (three.astype(f32) + one.astype(f32)) + (two.astype(f32) + total_b.astype(f32))
    own_cos = lax.dynamic_slice_in_dim(cosine, core * 64, 64, 0)
    own_sin = lax.dynamic_slice_in_dim(sine, core * 64, 64, 0)
    keys = rotate(total, own_cos, own_sin, 1.0).astype(bf16)
    keys = lax.all_gather(keys, "c", axis=0, tiled=True)

    grad_key_weight = jnp.sum(scattered.astype(f32), axis=0)
    return keys, grad_tokens, grad_key_weight


def solution(mesh):
    fine = Mesh(mesh.devices.reshape(2, 8, 8, 4, 2), ("zl", "y", "x", "zh", "c"))
    fsdp, tensor = ("zl", "y", "x"), ("zh", "c")
    placed = (P(fsdp, tensor), P(fsdp, None), P(fsdp, tensor), P(fsdp, None))
    return jax.shard_map(
        body,
        mesh=fine,
        in_specs=placed,
        out_specs=(P(fsdp, None), P(fsdp, tensor), P(fsdp, tensor)),
        check_vma=False,
    )
```

```python
import jax
import jax.numpy as jnp
from jax import lax
from jax.experimental import pallas as pl
from jax.experimental.pallas import tpu as pltpu
from jax.sharding import Mesh, PartitionSpec as P

HEAD = 128
SWAP = ((0, 1), (1, 0))


def doc_positions(segments):
    index = jnp.arange(segments.shape[0], dtype=jnp.int32)
    return index - jnp.sum((segments[None, :] < segments[:, None]).astype(jnp.int32), axis=1)


def angles(positions, half):
    freq = 500000.0 ** (-2.0 * jnp.arange(half, dtype=jnp.float32) / (2 * half))
    turn = positions.astype(jnp.float32)[:, None] * freq[None, :]
    return (jnp.cos(turn)[:, None, :], jnp.sin(turn)[:, None, :])


def rotate(field, cosine, sine, sign):
    rows = field.shape[0]
    shaped = field.reshape(rows, -1, HEAD)
    first, second = (shaped[..., : HEAD // 2], shaped[..., HEAD // 2 :])
    out = jnp.concatenate(
        [first * cosine - sign * second * sine, second * cosine + sign * first * sine], axis=-1
    )
    return out.reshape(rows, -1)


def dot(a, b, da, db):
    return lax.dot_general(a, b, (((da,), (db,)), ((), ())), preferred_element_type=jnp.float32)


def spread_kernel(w_ref, out_ref):
    out_ref[...] = jnp.broadcast_to(w_ref[...][None], out_ref.shape)


def kraw_kernel(tok_ref, par_ref, kb_ref, w_ref, keep_ref, send_ref, grad_ref):
    mine = pl.multiple_of(lax.axis_index("c") * 64, 64)
    other = pl.multiple_of(64 - mine, 64)
    halves = [ref[pl.ds(at, 64), :] for at in (mine, other) for ref in (tok_ref, par_ref)]
    out = dot(jnp.concatenate(halves, axis=0), w_ref[...], 1, 1)
    keep_ref[...] = out[:128]
    send_ref[...] = out[128:].astype(jnp.bfloat16)
    grad_ref[...] = dot(kb_ref[...], w_ref[...], 1, 0).astype(jnp.bfloat16)


def merge_kernel(keep_ref, c_ref, own_ref, far_ref):
    theirs = c_ref[1 - lax.axis_index("c")].astype(jnp.float32)
    out = (keep_ref[...] + theirs).astype(jnp.bfloat16)
    own_ref[...] = out[:64]
    far_ref[...] = out[64:]


def grad_kernel(kb_ref, w_ref, add_ref, out_ref):
    out = dot(kb_ref[...], w_ref[...], 1, 0) + add_ref[...].astype(jnp.float32)
    out_ref[...] = out.astype(jnp.bfloat16)


def whole(kernel, outs, n_in, name):
    vmem = pl.BlockSpec(memory_space=pltpu.VMEM)
    return pl.pallas_call(
        kernel,
        out_shape=outs,
        in_specs=[vmem] * n_in,
        out_specs=jax.tree.map(lambda _: vmem, outs),
        compiler_params=pltpu.CompilerParams(vmem_limit_bytes=12 << 20),
        name=name,
    )


def body(tokens, seg_ids, key_weight, key_grad):
    bf16, f32 = jnp.bfloat16, jnp.float32
    shape = jax.ShapeDtypeStruct
    zl, core = lax.axis_index("zl"), lax.axis_index("c")
    spread = whole(spread_kernel, shape((64, 4, 2048), bf16), 1, "spread")(key_weight)
    gathered = lax.all_to_all(spread, ("y", "x"), 0, 0)
    tok_p = lax.ppermute(tokens, "zl", SWAP)

    cosine, sine = angles(doc_positions(seg_ids[0]), HEAD // 2)
    kback = rotate(key_grad.astype(f32), cosine, sine, -1.0).astype(bf16)
    left, right = kback[:, :256], kback[:, 256:]
    kb_p = lax.ppermute(jnp.where(zl == 0, right, left), "zl", SWAP)
    kb = jnp.where(zl == 0, left, right)

    partial = (dot(kb, tokens, 0, 0) + dot(kb_p, tok_p, 0, 0)).astype(bf16).reshape(64, 4, 2048)

    weights = gathered.reshape(256, 2048)
    keep, to_c, g_send = whole(
        kraw_kernel,
        (shape((128, 256), f32), shape((128, 256), bf16), shape((128, 2048), bf16)),
        4,
        "kraw",
    )(tokens, tok_p, kb_p, weights)
    from_c = lax.all_gather(to_c, "c")
    half = shape((64, 256), bf16)
    own, to_z = whole(merge_kernel, (half, half), 2, "merge")(keep, from_c)
    from_z = lax.all_gather(to_z, "zl")
    scattered = lax.all_to_all(partial, ("y", "x"), 0, 0)

    total_b = jnp.where(
        zl == 0, jnp.concatenate([own, from_z[1]], 1), jnp.concatenate([from_z[0], own], 1)
    )
    total_b, g_send = lax.optimization_barrier((total_b, g_send))
    g_par = lax.ppermute(g_send, "zl", SWAP)
    one, three, two = (
        lax.ppermute(total_b, "zh", [(i, (i + step) % 4) for i in range(4)])
        for step in (1, 3, 2)
    )
    grad_tokens = whole(grad_kernel, shape((128, 2048), bf16), 3, "grad")(kb, weights, g_par)
    grad_key_weight = jnp.sum(scattered.astype(f32), axis=0)
    three, one, two, grad_tokens, grad_key_weight = lax.optimization_barrier(
        (three, one, two, grad_tokens, grad_key_weight)
    )
    total = (three.astype(f32) + one.astype(f32)) + (two.astype(f32) + total_b.astype(f32))
    own_cos = lax.dynamic_slice_in_dim(cosine, core * 64, 64, 0)
    own_sin = lax.dynamic_slice_in_dim(sine, core * 64, 64, 0)
    keys = rotate(total, own_cos, own_sin, 1.0).astype(bf16)
    keys = lax.all_gather(keys, "c", axis=0, tiled=True)

    return keys, grad_tokens, grad_key_weight


def solution(mesh):
    fine = Mesh(mesh.devices.reshape(2, 8, 8, 4, 2), ("zl", "y", "x", "zh", "c"))
    fsdp, tensor = ("zl", "y", "x"), ("zh", "c")
    placed = (P(fsdp, tensor), P(fsdp, None), P(fsdp, tensor), P(fsdp, None))
    return jax.shard_map(
        body,
        mesh=fine,
        in_specs=placed,
        out_specs=(P(fsdp, None), P(fsdp, tensor), P(fsdp, tensor)),
        check_vma=False,
    )
```

```python
import jax
import jax.numpy as jnp
from jax import lax
from jax.experimental import pallas as pl
from jax.experimental.pallas import tpu as pltpu
from jax.sharding import Mesh, PartitionSpec as P

HEAD = 128
SWAP = ((0, 1), (1, 0))


def doc_positions(segments):
    index = jnp.arange(segments.shape[0], dtype=jnp.int32)
    return index - jnp.sum((segments[None, :] < segments[:, None]).astype(jnp.int32), axis=1)


def angles(positions, half):
    freq = 500000.0 ** (-2.0 * jnp.arange(half, dtype=jnp.float32) / (2 * half))
    turn = positions.astype(jnp.float32)[:, None] * freq[None, :]
    return (jnp.cos(turn)[:, None, :], jnp.sin(turn)[:, None, :])


def rotate(field, cosine, sine, sign):
    rows = field.shape[0]
    shaped = field.reshape(rows, -1, HEAD)
    first, second = (shaped[..., : HEAD // 2], shaped[..., HEAD // 2 :])
    out = jnp.concatenate(
        [first * cosine - sign * second * sine, second * cosine + sign * first * sine], axis=-1
    )
    return out.reshape(rows, -1)


def dot(a, b, da, db):
    return lax.dot_general(a, b, (((da,), (db,)), ((), ())), preferred_element_type=jnp.float32)


def spread_kernel(w_ref, out_ref):
    out_ref[...] = jnp.broadcast_to(w_ref[...][None], out_ref.shape)


def kraw_kernel(tok_ref, par_ref, kb_ref, w_ref, keep_ref, send_ref, grad_ref):
    mine = pl.multiple_of(lax.axis_index("c") * 64, 64)
    other = pl.multiple_of(64 - mine, 64)
    halves = [ref[pl.ds(at, 64), :] for at in (mine, other) for ref in (tok_ref, par_ref)]
    out = dot(jnp.concatenate(halves, axis=0), w_ref[...], 1, 1)
    keep_ref[...] = out[:128]
    send_ref[...] = out[128:].astype(jnp.bfloat16)
    grad_ref[...] = dot(kb_ref[...], w_ref[...], 1, 0).astype(jnp.bfloat16)


def merge_kernel(keep_ref, c_ref, own_ref, far_ref):
    theirs = c_ref[1 - lax.axis_index("c")].astype(jnp.float32)
    out = (keep_ref[...] + theirs).astype(jnp.bfloat16)
    own_ref[...] = out[:64]
    far_ref[...] = out[64:]


def grad_kernel(kb_ref, w_ref, add_ref, out_ref):
    out = dot(kb_ref[...], w_ref[...], 1, 0) + add_ref[...].astype(jnp.float32)
    out_ref[...] = out.astype(jnp.bfloat16)


def whole(kernel, outs, n_in, name):
    vmem = pl.BlockSpec(memory_space=pltpu.VMEM)
    return pl.pallas_call(
        kernel,
        out_shape=outs,
        in_specs=[vmem] * n_in,
        out_specs=jax.tree.map(lambda _: vmem, outs),
        compiler_params=pltpu.CompilerParams(vmem_limit_bytes=12 << 20),
        name=name,
    )


def body(tokens, seg_ids, key_weight, key_grad):
    bf16, f32 = jnp.bfloat16, jnp.float32
    shape = jax.ShapeDtypeStruct
    zl, core = lax.axis_index("zl"), lax.axis_index("c")
    spread = whole(spread_kernel, shape((64, 4, 2048), bf16), 1, "spread")(key_weight)
    gathered = lax.all_to_all(spread, ("y", "x"), 0, 0)
    tok_p = lax.ppermute(tokens, "zl", SWAP)

    cosine, sine = angles(doc_positions(seg_ids[0]), HEAD // 2)
    kback = rotate(key_grad.astype(f32), cosine, sine, -1.0).astype(bf16)
    left, right = kback[:, :256], kback[:, 256:]
    kb_p = lax.ppermute(jnp.where(zl == 0, right, left), "zl", SWAP)
    kb = jnp.where(zl == 0, left, right)

    partial = (dot(kb, tokens, 0, 0) + dot(kb_p, tok_p, 0, 0)).astype(bf16).reshape(64, 4, 2048)

    weights = gathered.reshape(256, 2048)
    keep, to_c, g_send = whole(
        kraw_kernel,
        (shape((128, 256), f32), shape((128, 256), bf16), shape((128, 2048), bf16)),
        4,
        "kraw",
    )(tokens, tok_p, kb_p, weights)
    from_c = lax.all_gather(to_c, "c")
    half = shape((64, 256), bf16)
    own, to_z = whole(merge_kernel, (half, half), 2, "merge")(keep, from_c)
    from_z = lax.all_gather(to_z, "zl")
    scattered = lax.all_to_all(partial, ("y", "x"), 0, 0)

    total_b = jnp.where(
        zl == 0, jnp.concatenate([own, from_z[1]], 1), jnp.concatenate([from_z[0], own], 1)
    )
    g_par = lax.ppermute(g_send, "zl", SWAP)
    one, three, two = (
        lax.ppermute(total_b, "zh", [(i, (i + step) % 4) for i in range(4)])
        for step in (1, 3, 2)
    )
    grad_tokens = whole(grad_kernel, shape((128, 2048), bf16), 3, "grad")(kb, weights, g_par)
    grad_key_weight = jnp.sum(scattered.astype(f32), axis=0)
    three, one, two, grad_tokens, grad_key_weight = lax.optimization_barrier(
        (three, one, two, grad_tokens, grad_key_weight)
    )
    total = (three.astype(f32) + one.astype(f32)) + (two.astype(f32) + total_b.astype(f32))
    own_cos = lax.dynamic_slice_in_dim(cosine, core * 64, 64, 0)
    own_sin = lax.dynamic_slice_in_dim(sine, core * 64, 64, 0)
    keys = rotate(total, own_cos, own_sin, 1.0).astype(bf16)
    keys = lax.all_gather(keys, "c", axis=0, tiled=True)

    return keys, grad_tokens, grad_key_weight


def solution(mesh):
    fine = Mesh(mesh.devices.reshape(2, 8, 8, 4, 2), ("zl", "y", "x", "zh", "c"))
    fsdp, tensor = ("zl", "y", "x"), ("zh", "c")
    placed = (P(fsdp, tensor), P(fsdp, None), P(fsdp, tensor), P(fsdp, None))
    return jax.shard_map(
        body,
        mesh=fine,
        in_specs=placed,
        out_specs=(P(fsdp, None), P(fsdp, tensor), P(fsdp, tensor)),
        check_vma=False,
    )
```

```python
import jax
import jax.numpy as jnp
from jax import lax
from jax.experimental import pallas as pl
from jax.experimental.pallas import tpu as pltpu
from jax.sharding import Mesh, PartitionSpec as P

HEAD = 128
SWAP = ((0, 1), (1, 0))


def doc_positions(segments):
    index = jnp.arange(segments.shape[0], dtype=jnp.int32)
    return index - jnp.sum((segments[None, :] < segments[:, None]).astype(jnp.int32), axis=1)


def angles(positions, half):
    freq = 500000.0 ** (-2.0 * jnp.arange(half, dtype=jnp.float32) / (2 * half))
    turn = positions.astype(jnp.float32)[:, None] * freq[None, :]
    return (jnp.cos(turn)[:, None, :], jnp.sin(turn)[:, None, :])


def rotate(field, cosine, sine, sign):
    rows = field.shape[0]
    shaped = field.reshape(rows, -1, HEAD)
    first, second = (shaped[..., : HEAD // 2], shaped[..., HEAD // 2 :])
    out = jnp.concatenate(
        [first * cosine - sign * second * sine, second * cosine + sign * first * sine], axis=-1
    )
    return out.reshape(rows, -1)


def dot(a, b, da, db):
    return lax.dot_general(a, b, (((da,), (db,)), ((), ())), preferred_element_type=jnp.float32)


def spread_kernel(w_ref, out_ref):
    out_ref[...] = jnp.broadcast_to(w_ref[...][None], out_ref.shape)


def kraw_kernel(tok_ref, par_ref, kb_ref, w_ref, keep_ref, send_ref, a_ref, b_ref):
    mine = pl.multiple_of(lax.axis_index("c") * 64, 64)
    other = pl.multiple_of(64 - mine, 64)
    halves = [ref[pl.ds(at, 64), :] for at in (mine, other) for ref in (tok_ref, par_ref)]
    out = dot(jnp.concatenate(halves, axis=0), w_ref[...], 1, 1)
    keep_ref[...] = out[:128]
    send_ref[...] = out[128:].astype(jnp.bfloat16)
    grad = dot(kb_ref[...], w_ref[...], 1, 0).astype(jnp.bfloat16)
    a_ref[...] = grad[:, :1024]
    b_ref[...] = grad[:, 1024:]


def merge_kernel(keep_ref, c_ref, own_ref, far_ref):
    theirs = c_ref[1 - lax.axis_index("c")].astype(jnp.float32)
    out = (keep_ref[...] + theirs).astype(jnp.bfloat16)
    own_ref[...] = out[:64]
    far_ref[...] = out[64:]


def grad_kernel(kb_ref, w_ref, a_ref, b_ref, out_ref):
    out = dot(kb_ref[...], w_ref[...], 1, 0)
    out_ref[:, :1024] = (out[:, :1024] + a_ref[...].astype(jnp.float32)).astype(jnp.bfloat16)
    out_ref[:, 1024:] = (out[:, 1024:] + b_ref[...].astype(jnp.float32)).astype(jnp.bfloat16)


def whole(kernel, outs, n_in, name):
    vmem = pl.BlockSpec(memory_space=pltpu.VMEM)
    return pl.pallas_call(
        kernel,
        out_shape=outs,
        in_specs=[vmem] * n_in,
        out_specs=jax.tree.map(lambda _: vmem, outs),
        compiler_params=pltpu.CompilerParams(vmem_limit_bytes=12 << 20),
        name=name,
    )


def body(tokens, seg_ids, key_weight, key_grad):
    bf16, f32 = jnp.bfloat16, jnp.float32
    shape = jax.ShapeDtypeStruct
    zl, core = lax.axis_index("zl"), lax.axis_index("c")
    spread = whole(spread_kernel, shape((64, 4, 2048), bf16), 1, "spread")(key_weight)
    gathered = lax.all_to_all(spread, ("y", "x"), 0, 0)
    tok_p = lax.ppermute(tokens, "zl", SWAP)

    cosine, sine = angles(doc_positions(seg_ids[0]), HEAD // 2)
    kback = rotate(key_grad.astype(f32), cosine, sine, -1.0).astype(bf16)
    left, right = kback[:, :256], kback[:, 256:]
    kb_p = lax.ppermute(jnp.where(zl == 0, right, left), "zl", SWAP)
    kb = jnp.where(zl == 0, left, right)

    partial = (dot(kb, tokens, 0, 0) + dot(kb_p, tok_p, 0, 0)).astype(bf16).reshape(64, 4, 2048)

    weights = gathered.reshape(256, 2048)
    keep, to_c, a_send, b_send = whole(
        kraw_kernel,
        (shape((128, 256), f32), shape((128, 256), bf16)) + (shape((128, 1024), bf16),) * 2,
        4,
        "kraw",
    )(tokens, tok_p, kb_p, weights)
    from_c = lax.all_gather(to_c, "c")
    half = shape((64, 256), bf16)
    own, to_z = whole(merge_kernel, (half, half), 2, "merge")(keep, from_c)
    from_z = lax.all_gather(to_z, "zl")
    scattered = lax.all_to_all(partial, ("y", "x"), 0, 0)

    total_b = jnp.where(
        zl == 0, jnp.concatenate([own, from_z[1]], 1), jnp.concatenate([from_z[0], own], 1)
    )
    total_b, a_send, b_send = lax.optimization_barrier((total_b, a_send, b_send))
    a_par, b_par = lax.ppermute(a_send, "zl", SWAP), lax.ppermute(b_send, "zl", SWAP)
    one, three, two = (
        lax.ppermute(total_b, "zh", [(i, (i + step) % 4) for i in range(4)])
        for step in (1, 3, 2)
    )
    grad_key_weight = jnp.sum(scattered.astype(f32), axis=0)
    three, one, two, a_par, grad_key_weight = lax.optimization_barrier(
        (three, one, two, a_par, grad_key_weight)
    )
    total = (three.astype(f32) + one.astype(f32)) + (two.astype(f32) + total_b.astype(f32))
    own_cos = lax.dynamic_slice_in_dim(cosine, core * 64, 64, 0)
    own_sin = lax.dynamic_slice_in_dim(sine, core * 64, 64, 0)
    keys = rotate(total, own_cos, own_sin, 1.0).astype(bf16)
    keys = lax.all_gather(keys, "c", axis=0, tiled=True)

    grad_tokens = whole(grad_kernel, shape((128, 2048), bf16), 4, "grad")(kb, weights, a_par, b_par)
    return keys, grad_tokens, grad_key_weight


def solution(mesh):
    fine = Mesh(mesh.devices.reshape(2, 8, 8, 4, 2), ("zl", "y", "x", "zh", "c"))
    fsdp, tensor = ("zl", "y", "x"), ("zh", "c")
    placed = (P(fsdp, tensor), P(fsdp, None), P(fsdp, tensor), P(fsdp, None))
    return jax.shard_map(
        body,
        mesh=fine,
        in_specs=placed,
        out_specs=(P(fsdp, None), P(fsdp, tensor), P(fsdp, tensor)),
        check_vma=False,
    )
```
